32 devices in a mesh: rep: 2 (over x), row: 4 (over z), patch: 4 (over y, core).
Axes of the slice: x: 2, y: 2, z: 4, core: 2. Of those that a mesh axis runs over, the one named last changes fastest.
Arguments:
- tokens: bfloat16 [64, 64, 1152], P(('rep', 'row'), 'patch'), parts along dimension 0, may hold values from -6 to 6
- modulation: float32 [3, 1152], replicated, may hold values from -4 to 4
- w_query: bfloat16 [1152, 1152], replicated, may hold values from -1 to 1
- w_keyval: bfloat16 [1152, 2304], replicated, may hold values from -0.1875 to 0.1875
- w_out: bfloat16 [1152, 1152], replicated, may hold values from -0.1875 to 0.1875
- stale_kv: bfloat16 [32, 32, 2304], P(('rep', 'row'), 'patch'), parts along dimension 0, may hold values from -24 to 24, as said below
Outputs:
- block_out: bfloat16 [64, 64, 1152], P(('rep', 'row'), 'patch'), parts along dimension 0
- fresh_kv: bfloat16 [32, 32, 2304], P(('rep', 'row'), 'patch'), parts along dimension 0
The draws below stay inside these ranges and needn't reach their ends.
There are 2 independent parts, one for each index of `rep`. The reference program is written for one: setup_inputs(seed, part) draws one part's arguments, and reference() takes and returns one part's arrays. A program takes and returns all parts, laid end to end along the dimension named above; an argument that names none is the same for every part. Nothing has to cross between parts.
Inputs may be any that keep to these rules, and one draw needn't show every extreme that they name: `stale_kv`: pooled keys in the first 1152 entries of the last dimension, pooled values in the last 1152.
All inputs are finite; a program needn't handle non-finite values.
Results may differ from the reference program's by a relative error of at most 0.008.
Values may be sent and summed in bfloat16 or wider, within the bound.
A program may use at most 128 MiB of HBM per device.

```python
import math
import jax
import jax.numpy as jnp
from jax import lax

D = 1152
HEADS = 16
HEAD_DIM = 72
ROWS_DEV = 8
H = 32
W = 64
KEYS = 512
N_ROW = 4


def draw_stale_kv(key, part):
    key = jax.random.fold_in(key, 7)
    first = jax.random.fold_in(key, 0)
    base = 0.5 * jax.random.normal(first, (H // 2, W // 2, 2 * D), jnp.float32)
    return jnp.clip(base, -24.0, 24.0).astype(jnp.bfloat16)


def shard_levels(key, shape, shards, smallest, high):
    gain = 1.0
    for dim, shards_of in shards:
        steps = jax.random.uniform(jax.random.fold_in(jax.random.fold_in(key, 6), dim), (shards_of,), jnp.float32, smallest / len(shards), high / len(shards))
        gain = gain * jnp.repeat(jnp.exp(steps), shape[dim] // shards_of).reshape((-1,) + (1,) * (len(shape) - 1 - dim))
    return gain


def bell_draw(rng, extent, scale, bound, cuts=(), kind=jnp.bfloat16):
    entries = scale * jax.random.normal(rng, extent, jnp.float32)
    if cuts:
        entries = entries * shard_levels(rng, extent, cuts, -0.22, 0.18)
    return jnp.clip(entries, -bound, bound).astype(kind)


def setup_inputs(seed: int = 0, part: int = 0) -> dict:
    seeds = jax.random.split(jax.random.key(seed), 7)
    own_keys = jax.random.split(jax.random.fold_in(seeds[6], part), 7)
    return {
        "tokens": bell_draw(own_keys[0], (H, W, D), 1.0, 6.0, ((0, 4), (1, 4))),
        "modulation": bell_draw(seeds[1], (3, D), 0.7, 4.0, (), jnp.float32),
        "w_query": bell_draw(seeds[2], (D, D), (D // 36) ** -0.5, 1.0),
        "w_keyval": bell_draw(seeds[3], (D, 2 * D), D ** -0.5, 0.1875),
        "w_out": bell_draw(seeds[4], (D, D), D ** -0.5, 0.1875),
        "stale_kv": draw_stale_kv(jax.random.fold_in(jax.random.fold_in(seeds[6], part), 71), part),
    }


def modulate(tokens, modulation):
    values = tokens.astype(jnp.float32)
    center = lax.optimization_barrier(jnp.mean(values, axis=-1, keepdims=True))
    spread = lax.optimization_barrier(jnp.mean((values - center) ** 2, axis=-1, keepdims=True))
    normal = (values - center) / jnp.sqrt(spread + 1e-06)
    return (normal * (1.0 + modulation[1]) + modulation[0]).astype(jnp.bfloat16)

def reference(tokens, modulation, w_query, w_keyval, w_out, stale_kv):
    normed = modulate(tokens, modulation).reshape(H * W, D)
    query = jnp.dot(normed, w_query, preferred_element_type=jnp.float32).astype(jnp.bfloat16)
    keyval = jnp.dot(normed, w_keyval, preferred_element_type=jnp.float32)
    fresh_kv = keyval.reshape(H // 2, 2, W // 2, 2, 2 * D).mean(axis=(1, 3)).astype(jnp.bfloat16)
    pooled_group = (jnp.arange(H // 2) // (ROWS_DEV // 2)).astype(jnp.int32)
    group_tokens = ROWS_DEV * W
    block = math.gcd(group_tokens, 512)
    query_groups = query.reshape(N_ROW, group_tokens // block, block, HEADS, HEAD_DIM)
    scale = 1.0 / math.sqrt(HEAD_DIM)

    def one_group(index):
        chosen = (pooled_group == index)[:, None, None]
        used = jnp.where(chosen, fresh_kv, stale_kv).reshape(KEYS, 2 * D)
        keys = used[:, :D].reshape(KEYS, HEADS, HEAD_DIM).astype(jnp.float32)
        values = used[:, D:].reshape(KEYS, HEADS, HEAD_DIM).astype(jnp.float32)
        blocks = lax.dynamic_index_in_dim(query_groups, index, 0, keepdims=False)

        def one_block(queries):
            scores = jnp.einsum('thd,nhd->htn', queries.astype(jnp.float32), keys) * scale
            top = lax.optimization_barrier(jnp.max(scores, axis=-1, keepdims=True))
            expo = jnp.exp(scores - top)
            total = lax.optimization_barrier(jnp.sum(expo, axis=-1))
            weights = expo.astype(jnp.bfloat16).astype(jnp.float32)
            summed = jnp.einsum('htn,nhd->thd', weights, values)
            return (summed / jnp.transpose(total)[:, :, None]).astype(jnp.bfloat16)
        return lax.map(one_block, blocks)
    attended = lax.map(one_group, jnp.arange(N_ROW, dtype=jnp.int32)).reshape(H * W, D)
    projected = jnp.dot(attended, w_out, preferred_element_type=jnp.float32)
    block_out = tokens.reshape(H * W, D).astype(jnp.float32) + modulation[2] * projected
    return (block_out.astype(jnp.bfloat16).reshape(H, W, D), fresh_kv)
```

```python
import functools
import math

import jax
import jax.numpy as jnp
from jax import lax
from jax.experimental import pallas as pl
from jax.experimental.pallas import tpu as pltpu
from jax.sharding import PartitionSpec as P

HEADS = 16
HEAD_DIM = 72
PAIRS = HEADS // 2
LANES = 128
WINDOW = 256
MESH = pl.DeviceIdType.MESH
F32 = jnp.float32
BF16 = jnp.bfloat16
KV_PARTS = 3
Q_PARTS = 3


def kernel(
    n_row, n_patch, grid_cols,
    tok_hbm, mod_hbm, wq_hbm, wkv_hbm, wo_hbm, stale_hbm,
    out_ref, fresh_hbm,
    tok, mod, wq, wkv, wo, kv, normed, pair_q, top, total, summed, attended,
    load_sem, kv_sem, recv_sem, first_sem, z_sem, y_sem, core_sem, fresh_sem,
):
    tokens, width = tok.shape
    block = stale_hbm.shape[0]
    n_y = n_patch // 2
    row = lax.axis_index("row")
    patch = lax.axis_index("patch")
    y_own = patch // 2
    core = patch % 2
    sibling = patch + 1 - 2 * core

    def slot(group, column):
        start = pl.multiple_of((group * n_patch + column) * block, block)
        return kv.at[pl.ds(start, block), :]

    def send(src, group, column, sem, target):
        return pltpu.make_async_remote_copy(
            src_ref=src, dst_ref=slot(group, column), send_sem=sem,
            recv_sem=recv_sem.at[group, column], device_id=target, device_id_type=MESH,
        )

    def arrived(group, column):
        pltpu.make_async_copy(
            slot(group, column), slot(group, column), recv_sem.at[group, column]
        ).wait()

    def y_column(step):
        return lax.rem(y_own + step, n_y) * 2 + core

    near = jnp.minimum(row, n_row - 1 - row)
    lower = row > n_row - 1 - row

    def order(k):
        both = k < 2 * near
        step = jnp.where(both, k // 2 + 1, k - near + 1)
        down = jnp.where(both, k % 2 == 0, lower)
        return jnp.where(down, row - step, row + step)

    loads = [
        pltpu.make_async_copy(tok_hbm, tok, load_sem.at[0]),
        pltpu.make_async_copy(mod_hbm, mod, load_sem.at[1]),
    ]
    kv_width = 2 * width // KV_PARTS
    kv_loads = [
        pltpu.make_async_copy(
            wkv_hbm.at[:, pl.ds(i * kv_width, kv_width)],
            wkv.at[:, pl.ds(i * kv_width, kv_width)],
            kv_sem.at[i],
        )
        for i in range(KV_PARTS)
    ]
    wq_load = pltpu.make_async_copy(wq_hbm, wq, load_sem.at[2])
    wo_load = pltpu.make_async_copy(wo_hbm, wo, load_sem.at[3])
    for item in loads + kv_loads + [wq_load, wo_load]:
        item.start()

    barrier = pltpu.get_barrier_semaphore()

    @pl.when(row > 0)
    def _():
        pl.semaphore_signal(barrier, inc=1, device_id={"row": row - 1}, device_id_type=MESH)

    @pl.when(row < n_row - 1)
    def _():
        pl.semaphore_signal(barrier, inc=1, device_id={"row": row + 1}, device_id_type=MESH)

    for step in range(1, n_y):
        pl.semaphore_signal(
            barrier, inc=1, device_id={"patch": y_column(step)}, device_id_type=MESH
        )
    pl.semaphore_signal(barrier, inc=1, device_id={"patch": sibling}, device_id_type=MESH)
    pl.semaphore_wait(
        barrier,
        n_y + jnp.where(row > 0, 1, 0) + jnp.where(row < n_row - 1, 1, 0),
    )

    first_down = send(stale_hbm, row, patch, first_sem.at[0], {"row": row - 1})
    first_up = send(stale_hbm, row, patch, first_sem.at[1], {"row": row + 1})

    @pl.when(row > 0)
    def _():
        first_down.start()

    @pl.when(row < n_row - 1)
    def _():
        first_up.start()

    def spread(group):
        for step in range(1, n_y):
            send(slot(group, patch), group, patch, y_sem.at[group, step],
                 {"patch": y_column(step)}).start()
        send(slot(group, patch), group, patch, core_sem.at[group, 0], {"patch": sibling}).start()

    def spread_wait(group):
        for step in range(1, n_y):
            send(slot(group, patch), group, patch, y_sem.at[group, step],
                 {"patch": y_column(step)}).wait_send()
        for step in range(n_y):
            send(slot(group, patch), group, patch, core_sem.at[group, step],
                 {"patch": sibling}).wait_send()

    def passed(k):
        group = order(k)
        target = jnp.where(group < row, row + 1, row - 1)
        copy = send(slot(group, patch), group, patch, z_sem.at[k], {"row": target})
        return group, (target >= 0) & (target < n_row), copy

    def row_event(k):
        group, inside, copy = passed(k)
        arrived(group, patch)

        @pl.when(inside)
        def _():
            copy.start()

        spread(group)

    def relay(group):
        for step in range(1, n_y):
            column = y_column(step)
            arrived(group, column)
            send(slot(group, column), group, column, core_sem.at[group, step],
                 {"patch": sibling}).start()

    def gathered(group):
        for step in range(n_y):
            arrived(group, y_column(step) + 1 - 2 * core)

    for item in loads:
        item.wait()
    values = tok[...].astype(F32)
    center = jnp.mean(values, axis=-1, keepdims=True)
    offset = values - center
    spread_sq = jnp.mean(offset * offset, axis=-1, keepdims=True)
    normal = offset * lax.rsqrt(spread_sq + 1e-06)
    normed[...] = (normal * (1.0 + mod[1:2, :]) + mod[0:1, :]).astype(BF16)

    cell = lax.broadcasted_iota(jnp.int32, (block, tokens), 0)
    token = lax.broadcasted_iota(jnp.int32, (block, tokens), 1)
    home = (token // (2 * grid_cols)) * (grid_cols // 2) + (token % grid_cols) // 2
    pool = jnp.where(home == cell, 0.25, 0.0).astype(BF16)
    pooled = jnp.dot(pool, normed[...], preferred_element_type=F32)
    coarse = pooled.astype(BF16)
    fine = (pooled - coarse.astype(F32)).astype(BF16)
    both_parts = jnp.concatenate([coarse, fine], axis=0)
    own = slot(row, patch)
    for i in range(KV_PARTS):
        kv_loads[i].wait()
        columns = pl.ds(i * kv_width, kv_width)
        product = jnp.dot(both_parts, wkv[:, columns], preferred_element_type=F32)
        own[:, columns] = (product[:block] + product[block:]).astype(BF16)
    spread(row)
    fresh_copy = pltpu.make_async_copy(own, fresh_hbm, fresh_sem)
    fresh_copy.start()

    if n_row > 1:
        row_event(0)

    wq_load.wait()
    lane = lax.broadcasted_iota(jnp.int32, (tokens, WINDOW), 1)

    def in_head(pair, which):
        begin = pair * (2 * HEAD_DIM - LANES) + which * HEAD_DIM
        return (lane >= begin) & (lane < begin + HEAD_DIM)

    query = jnp.dot(normed[...], wq[...], preferred_element_type=F32)
    for pair in range(PAIRS):
        window = query[:, pair * LANES : pair * LANES + WINDOW]
        for which in range(2):
            pair_q[pair, which * tokens : (which + 1) * tokens, :] = jnp.where(
                in_head(pair, which), window, 0.0
            ).astype(BF16)

    top[...] = jnp.full(top.shape, -1e30, F32)
    total[...] = jnp.zeros(total.shape, F32)
    summed[...] = jnp.zeros(summed.shape, F32)
    factor = math.log2(math.e) / math.sqrt(HEAD_DIM)

    def attend(start):
        rows = pl.ds(pl.multiple_of(start, LANES), LANES)
        for pair in range(PAIRS):
            keys = kv[rows, pair * LANES : pair * LANES + WINDOW]
            vals = kv[rows, width + pair * LANES : width + pair * LANES + WINDOW]
            scores = lax.dot_general(
                pair_q[pair], keys, (((1,), (1,)), ((), ())), preferred_element_type=F32
            )
            before = top[pair]
            newest = jnp.maximum(before, jnp.max(scores, axis=-1, keepdims=True))
            top[pair] = newest
            scale = jnp.exp2((before - newest) * factor)
            expo = jnp.exp2((scores - newest) * factor)
            total[pair] = total[pair] * scale + expo
            added = jnp.dot(expo.astype(BF16), vals, preferred_element_type=F32)
            summed[pair] = summed[pair] * jnp.concatenate([scale, scale], axis=1) + added

    group_rows = n_patch * block

    def step_group(q, carry):
        group = jnp.where(q == 0, row, order(jnp.maximum(q - 1, 0)))
        relay(group)

        @pl.when(q + 1 < n_row - 1)
        def _():
            row_event(q + 1)

        gathered(group)

        def step_part(u, state):
            attend(group * group_rows + u * LANES)
            return state

        return lax.fori_loop(0, group_rows // LANES, step_part, carry)

    lax.fori_loop(0, n_row, step_group, 0)

    attended[...] = jnp.zeros(attended.shape, F32)
    for pair in range(PAIRS):
        scaled = summed[pair] * (1.0 / jnp.sum(total[pair], axis=-1, keepdims=True))
        columns = slice(pair * LANES, pair * LANES + WINDOW)
        attended[:, columns] += jnp.where(
            in_head(pair, 0), scaled[:tokens], jnp.where(in_head(pair, 1), scaled[tokens:], 0.0)
        )
    wo_load.wait()
    heads = attended[...].astype(BF16)
    projected = jnp.dot(heads, wo[...], preferred_element_type=F32)
    out_ref[...] = (tok[...].astype(F32) + mod[2:3, :] * projected).astype(BF16)

    @pl.when(row > 0)
    def _():
        first_down.wait_send()

    @pl.when(row < n_row - 1)
    def _():
        first_up.wait_send()

    def finish(k, carry):
        group, inside, copy = passed(k)

        @pl.when(inside)
        def _():
            copy.wait_send()

        spread_wait(group)
        return carry

    lax.fori_loop(0, n_row - 1, finish, 0)
    spread_wait(row)
    fresh_copy.wait()


def on_device(n_row, n_patch, tokens, modulation, w_query, w_keyval, w_out, stale_kv):
    grid_rows, grid_cols, width = tokens.shape
    count = grid_rows * grid_cols
    block = count // 4
    dma = pltpu.SemaphoreType.DMA
    out, fresh = pl.pallas_call(
        functools.partial(kernel, n_row, n_patch, grid_cols),
        out_shape=(
            jax.ShapeDtypeStruct((count, width), BF16),
            jax.ShapeDtypeStruct((block, 2 * width), BF16),
        ),
        in_specs=[pl.BlockSpec(memory_space=pl.ANY)] * 6,
        out_specs=(
            pl.BlockSpec(memory_space=pltpu.VMEM),
            pl.BlockSpec(memory_space=pl.ANY),
        ),
        scratch_shapes=[
            pltpu.VMEM((count, width), BF16),
            pltpu.VMEM(modulation.shape, F32),
            pltpu.VMEM((width, width), BF16),
            pltpu.VMEM((width, 2 * width), BF16),
            pltpu.VMEM((width, width), BF16),
            pltpu.VMEM((n_row * n_patch * block, 2 * width), BF16),
            pltpu.VMEM((count, width), BF16),
            pltpu.VMEM((PAIRS, 2 * count, WINDOW), BF16),
            pltpu.VMEM((PAIRS, 2 * count, LANES), F32),
            pltpu.VMEM((PAIRS, 2 * count, LANES), F32),
            pltpu.VMEM((PAIRS, 2 * count, WINDOW), F32),
            pltpu.VMEM((count, width), F32),
            dma((4,)),
            dma((KV_PARTS,)),
            dma((n_row, n_patch)),
            dma((2,)),
            dma((n_row,)),
            dma((n_row, n_patch // 2)),
            dma((n_row, n_patch // 2)),
            dma(()),
        ],
        compiler_params=pltpu.CompilerParams(
            collective_id=0, has_side_effects=True, vmem_limit_bytes=56 * 1024 * 1024
        ),
    )(
        tokens.reshape(count, width), modulation, w_query, w_keyval, w_out,
        stale_kv.reshape(block, 2 * width),
    )
    return out.reshape(tokens.shape), fresh.reshape(stale_kv.shape)


def solution(mesh):
    tiled = P(("rep", "row"), "patch", None)
    return jax.shard_map(
        functools.partial(on_device, mesh.shape["row"], mesh.shape["patch"]),
        mesh=mesh,
        in_specs=(tiled, P(), P(), P(), P(), tiled),
        out_specs=(tiled, tiled),
        check_vma=False,
    )
```

```python
import functools
import math

import jax
import jax.numpy as jnp
from jax import lax
from jax.experimental import pallas as pl
from jax.experimental.pallas import tpu as pltpu
from jax.sharding import PartitionSpec as P

HEADS = 16
HEAD_DIM = 72
PAIRS = HEADS // 2
LANES = 128
WINDOW = 256
MESH = pl.DeviceIdType.MESH
F32 = jnp.float32
BF16 = jnp.bfloat16
KV_PARTS = 3
Q_PARTS = 3


def kernel(
    n_row, n_patch, grid_cols,
    tok_hbm, mod_hbm, wq_hbm, wkv_hbm, wo_hbm, stale_hbm,
    out_ref, fresh_hbm,
    tok, mod, wq, wkv, wo, kv, normed, pair_q, top, total, summed, attended,
    load_sem, kv_sem, recv_sem, first_sem, z_sem, y_sem, core_sem, fresh_sem,
):
    tokens, width = tok.shape
    block = stale_hbm.shape[0]
    n_y = n_patch // 2
    row = lax.axis_index("row")
    patch = lax.axis_index("patch")
    y_own = patch // 2
    core = patch % 2
    sibling = patch + 1 - 2 * core

    def slot(group, column):
        start = pl.multiple_of((group * n_patch + column) * block, block)
        return kv.at[pl.ds(start, block), :]

    def send(src, group, column, sem, target):
        return pltpu.make_async_remote_copy(
            src_ref=src, dst_ref=slot(group, column), send_sem=sem,
            recv_sem=recv_sem.at[group, column], device_id=target, device_id_type=MESH,
        )

    def arrived(group, column):
        pltpu.make_async_copy(
            slot(group, column), slot(group, column), recv_sem.at[group, column]
        ).wait()

    def y_column(step):
        return lax.rem(y_own + step, n_y) * 2 + core

    near = jnp.minimum(row, n_row - 1 - row)
    lower = row > n_row - 1 - row

    def order(k):
        both = k < 2 * near
        step = jnp.where(both, k // 2 + 1, k - near + 1)
        down = jnp.where(both, k % 2 == 0, lower)
        return jnp.where(down, row - step, row + step)

    barrier = pltpu.get_barrier_semaphore()

    @pl.when(row > 0)
    def _():
        pl.semaphore_signal(barrier, inc=1, device_id={"row": row - 1}, device_id_type=MESH)

    @pl.when(row < n_row - 1)
    def _():
        pl.semaphore_signal(barrier, inc=1, device_id={"row": row + 1}, device_id_type=MESH)

    for step in range(1, n_y):
        pl.semaphore_signal(
            barrier, inc=1, device_id={"patch": y_column(step)}, device_id_type=MESH
        )
    pl.semaphore_signal(barrier, inc=1, device_id={"patch": sibling}, device_id_type=MESH)
    loads = [
        pltpu.make_async_copy(tok_hbm, tok, load_sem.at[0]),
        pltpu.make_async_copy(mod_hbm, mod, load_sem.at[1]),
    ]
    kv_width = 2 * width // KV_PARTS
    kv_loads = [
        pltpu.make_async_copy(
            wkv_hbm.at[:, pl.ds(i * kv_width, kv_width)],
            wkv.at[:, pl.ds(i * kv_width, kv_width)],
            kv_sem.at[i],
        )
        for i in range(KV_PARTS)
    ]
    wq_load = pltpu.make_async_copy(wq_hbm, wq, load_sem.at[2])
    wo_load = pltpu.make_async_copy(wo_hbm, wo, load_sem.at[3])
    for item in loads + kv_loads + [wq_load, wo_load]:
        item.start()

    pl.semaphore_wait(
        barrier,
        n_y + jnp.where(row > 0, 1, 0) + jnp.where(row < n_row - 1, 1, 0),
    )

    first_down = send(stale_hbm, row, patch, first_sem.at[0], {"row": row - 1})
    first_up = send(stale_hbm, row, patch, first_sem.at[1], {"row": row + 1})

    @pl.when(row > 0)
    def _():
        first_down.start()

    @pl.when(row < n_row - 1)
    def _():
        first_up.start()

    def spread(group):
        for step in range(1, n_y):
            send(slot(group, patch), group, patch, y_sem.at[group, step],
                 {"patch": y_column(step)}).start()
        send(slot(group, patch), group, patch, core_sem.at[group, 0], {"patch": sibling}).start()

    def spread_wait(group):
        for step in range(1, n_y):
            send(slot(group, patch), group, patch, y_sem.at[group, step],
                 {"patch": y_column(step)}).wait_send()
        for step in range(n_y):
            send(slot(group, patch), group, patch, core_sem.at[group, step],
                 {"patch": sibling}).wait_send()

    def passed(distance, sign, act):
        group = row + sign * distance
        target = row - sign

        @pl.when((group >= 0) & (group < n_row))
        def _():
            copy = send(slot(group, patch), group, patch, z_sem.at[group], {"row": target})
            act(group, (target >= 0) & (target < n_row), copy)

    def row_event(distance):
        def act(group, inside, copy):
            arrived(group, patch)

            @pl.when(inside)
            def _():
                copy.start()

            spread(group)

        passed(distance, 1, act)
        passed(distance, -1, act)

    def relay(group):
        for step in range(1, n_y):
            column = y_column(step)
            arrived(group, column)
            send(slot(group, column), group, column, core_sem.at[group, step],
                 {"patch": sibling}).start()

    def gathered(group):
        for step in range(n_y):
            arrived(group, y_column(step) + 1 - 2 * core)

    for item in loads:
        item.wait()
    values = tok[...].astype(F32)
    center = jnp.mean(values, axis=-1, keepdims=True)
    offset = values - center
    spread_sq = jnp.mean(offset * offset, axis=-1, keepdims=True)
    normal = offset * lax.rsqrt(spread_sq + 1e-06)
    normed[...] = (normal * (1.0 + mod[1:2, :]) + mod[0:1, :]).astype(BF16)

    cell = lax.broadcasted_iota(jnp.int32, (block, tokens), 0)
    token = lax.broadcasted_iota(jnp.int32, (block, tokens), 1)
    home = (token // (2 * grid_cols)) * (grid_cols // 2) + (token % grid_cols) // 2
    pool = jnp.where(home == cell, 0.25, 0.0).astype(BF16)
    pooled = jnp.dot(pool, normed[...], preferred_element_type=F32)
    coarse = pooled.astype(BF16)
    fine = (pooled - coarse.astype(F32)).astype(BF16)
    both_parts = jnp.concatenate([coarse, fine], axis=0)
    own = slot(row, patch)
    for i in range(KV_PARTS):
        kv_loads[i].wait()
        columns = pl.ds(i * kv_width, kv_width)
        product = jnp.dot(both_parts, wkv[:, columns], preferred_element_type=F32)
        own[:, columns] = (product[:block] + product[block:]).astype(BF16)
    spread(row)
    fresh_copy = pltpu.make_async_copy(own, fresh_hbm, fresh_sem)
    fresh_copy.start()

    if n_row > 1:
        row_event(1)

    wq_load.wait()
    lane = lax.broadcasted_iota(jnp.int32, (tokens, WINDOW), 1)

    def in_head(pair, which):
        begin = pair * (2 * HEAD_DIM - LANES) + which * HEAD_DIM
        return (lane >= begin) & (lane < begin + HEAD_DIM)

    query = jnp.dot(normed[...], wq[...], preferred_element_type=F32)
    for pair in range(PAIRS):
        window = query[:, pair * LANES : pair * LANES + WINDOW]
        for which in range(2):
            pair_q[pair, which * tokens : (which + 1) * tokens, :] = jnp.where(
                in_head(pair, which), window, 0.0
            ).astype(BF16)

    top[...] = jnp.full(top.shape, -1e30, F32)
    total[...] = jnp.zeros(total.shape, F32)
    summed[...] = jnp.zeros(summed.shape, F32)
    factor = math.log2(math.e) / math.sqrt(HEAD_DIM)

    def attend(start):
        rows = pl.ds(pl.multiple_of(start, LANES), LANES)
        for pair in range(PAIRS):
            keys = kv[rows, pair * LANES : pair * LANES + WINDOW]
            vals = kv[rows, width + pair * LANES : width + pair * LANES + WINDOW]
            scores = lax.dot_general(
                pair_q[pair], keys, (((1,), (1,)), ((), ())), preferred_element_type=F32
            )
            before = top[pair]
            newest = jnp.maximum(before, jnp.max(scores, axis=-1, keepdims=True))
            top[pair] = newest
            scale = jnp.exp2((before - newest) * factor)
            expo = jnp.exp2((scores - newest) * factor)
            total[pair] = total[pair] * scale + expo
            added = jnp.dot(expo.astype(BF16), vals, preferred_element_type=F32)
            summed[pair] = summed[pair] * jnp.concatenate([scale, scale], axis=1) + added

    group_rows = n_patch * block

    def step_group(q, carry):
        group = jnp.where(q == 0, row, order(jnp.maximum(q - 1, 0)))
        relay(group)

        @pl.when(q + 2 < n_row)
        def _():
            row_event(q + 2)

        gathered(group)

        def step_part(u, state):
            attend(group * group_rows + u * LANES)
            return state

        return lax.fori_loop(0, group_rows // LANES, step_part, carry)

    lax.fori_loop(0, n_row, step_group, 0)

    attended[...] = jnp.zeros(attended.shape, F32)
    for pair in range(PAIRS):
        scaled = summed[pair] * (1.0 / jnp.sum(total[pair], axis=-1, keepdims=True))
        columns = slice(pair * LANES, pair * LANES + WINDOW)
        attended[:, columns] += jnp.where(
            in_head(pair, 0), scaled[:tokens], jnp.where(in_head(pair, 1), scaled[tokens:], 0.0)
        )
    wo_load.wait()
    heads = attended[...].astype(BF16)
    projected = jnp.dot(heads, wo[...], preferred_element_type=F32)
    out_ref[...] = (tok[...].astype(F32) + mod[2:3, :] * projected).astype(BF16)

    @pl.when(row > 0)
    def _():
        first_down.wait_send()

    @pl.when(row < n_row - 1)
    def _():
        first_up.wait_send()

    def finish(distance, carry):
        def act(group, inside, copy):
            @pl.when(inside)
            def _():
                copy.wait_send()

            spread_wait(group)

        passed(distance, 1, act)
        passed(distance, -1, act)
        return carry

    lax.fori_loop(1, n_row, finish, 0)
    spread_wait(row)
    fresh_copy.wait()


def place(first, second, first_out, second_out, first_held, second_held, sem):
    loads = [
        pltpu.make_async_copy(first, first_held, sem.at[0]),
        pltpu.make_async_copy(second, second_held, sem.at[1]),
    ]
    stores = [
        pltpu.make_async_copy(first_held, first_out, sem.at[2]),
        pltpu.make_async_copy(second_held, second_out, sem.at[3]),
    ]
    for item in loads:
        item.start()
    for load, store in zip(loads, stores):
        load.wait()
        store.start()
    for item in stores:
        item.wait()


def on_device(n_row, n_patch, tokens, modulation, w_query, w_keyval, w_out, stale_kv):
    grid_rows, grid_cols, width = tokens.shape
    count = grid_rows * grid_cols
    block = count // 4
    dma = pltpu.SemaphoreType.DMA
    out, fresh = pl.pallas_call(
        functools.partial(kernel, n_row, n_patch, grid_cols),
        out_shape=(
            jax.ShapeDtypeStruct((count, width), BF16),
            jax.ShapeDtypeStruct((block, 2 * width), BF16),
        ),
        in_specs=[pl.BlockSpec(memory_space=pl.ANY)] * 6,
        out_specs=(
            pl.BlockSpec(memory_space=pltpu.VMEM),
            pl.BlockSpec(memory_space=pl.ANY),
        ),
        scratch_shapes=[
            pltpu.VMEM((count, width), BF16),
            pltpu.VMEM(modulation.shape, F32),
            pltpu.VMEM((width, width), BF16),
            pltpu.VMEM((width, 2 * width), BF16),
            pltpu.VMEM((width, width), BF16),
            pltpu.VMEM((n_row * n_patch * block, 2 * width), BF16),
            pltpu.VMEM((count, width), BF16),
            pltpu.VMEM((PAIRS, 2 * count, WINDOW), BF16),
            pltpu.VMEM((PAIRS, 2 * count, LANES), F32),
            pltpu.VMEM((PAIRS, 2 * count, LANES), F32),
            pltpu.VMEM((PAIRS, 2 * count, WINDOW), F32),
            pltpu.VMEM((count, width), F32),
            dma((4,)),
            dma((KV_PARTS,)),
            dma((n_row, n_patch)),
            dma((2,)),
            dma((n_row,)),
            dma((n_row, n_patch // 2)),
            dma((n_row, n_patch // 2)),
            dma(()),
        ],
        compiler_params=pltpu.CompilerParams(
            collective_id=0, has_side_effects=True, vmem_limit_bytes=56 * 1024 * 1024
        ),
    )(
        tokens.reshape(count, width), modulation, w_query, w_keyval, w_out,
        stale_kv.reshape(block, 2 * width),
    )
    hbm = pl.BlockSpec(memory_space=pl.ANY)
    out, fresh = pl.pallas_call(
        place,
        out_shape=(
            jax.ShapeDtypeStruct(out.shape, BF16),
            jax.ShapeDtypeStruct(fresh.shape, BF16),
        ),
        in_specs=[hbm, hbm],
        out_specs=(hbm, hbm),
        scratch_shapes=[pltpu.VMEM(out.shape, BF16), pltpu.VMEM(fresh.shape, BF16), dma((4,))],
        compiler_params=pltpu.CompilerParams(vmem_limit_bytes=56 * 1024 * 1024),
    )(out, fresh)
    return out.reshape(tokens.shape), fresh.reshape(stale_kv.shape)


def solution(mesh):
    tiled = P(("rep", "row"), "patch", None)
    return jax.shard_map(
        functools.partial(on_device, mesh.shape["row"], mesh.shape["patch"]),
        mesh=mesh,
        in_specs=(tiled, P(), P(), P(), P(), tiled),
        out_specs=(tiled, tiled),
        check_vma=False,
    )
```

```python
import functools
import math

import jax
import jax.numpy as jnp
from jax import lax
from jax.experimental import pallas as pl
from jax.experimental.pallas import tpu as pltpu
from jax.sharding import PartitionSpec as P

HEADS = 16
HEAD_DIM = 72
PAIRS = HEADS // 2
LANES = 128
WINDOW = 256
MESH = pl.DeviceIdType.MESH
F32 = jnp.float32
BF16 = jnp.bfloat16
KV_PARTS = 3


def kernel(
    n_row, n_patch, grid_cols,
    tok_hbm, mod_hbm, wq_hbm, wkv_hbm, wo_hbm, stale_hbm,
    out_ref, fresh_hbm,
    tok, mod, wq, wkv, wo, kv, normed, pair_q, top, total, summed, attended,
    cross, load_sem, kv_sem, recv_sem, key_sem, cross_recv, cross_send, pass_sem, first_sem, z_sem, y_sem, core_sem, fresh_sem,
):
    tokens, width = tok.shape
    block = stale_hbm.shape[0]
    n_y = n_patch // 2
    row = lax.axis_index("row")
    patch = lax.axis_index("patch")
    y_own = patch // 2
    core = patch % 2
    sibling = patch + 1 - 2 * core

    def slot(group, column):
        start = pl.multiple_of((group * n_patch + column) * block, block)
        return kv.at[pl.ds(start, block), :]

    def send(src, group, column, sem, target):
        return pltpu.make_async_remote_copy(
            src_ref=src, dst_ref=slot(group, column), send_sem=sem,
            recv_sem=recv_sem.at[group, column], device_id=target, device_id_type=MESH,
        )

    def arrived(group, column):
        pltpu.make_async_copy(
            slot(group, column), slot(group, column), recv_sem.at[group, column]
        ).wait()

    def half(ref, which):
        return ref.at[:, pl.ds(which * width, width)]

    def cross_send_copy(step):
        return pltpu.make_async_remote_copy(
            src_ref=half(stale_hbm, 0), dst_ref=cross.at[y_own], send_sem=cross_send.at[step],
            recv_sem=cross_recv.at[y_own], device_id={"patch": y_column(step)},
            device_id_type=MESH,
        )

    def cross_pass(step, target, which):
        column = y_column(step)
        return pltpu.make_async_remote_copy(
            src_ref=cross.at[column // 2], dst_ref=half(slot(row, column), 0),
            send_sem=pass_sem.at[which, step], recv_sem=key_sem.at[row, column],
            device_id={"row": target}, device_id_type=MESH,
        )

    def cross_event(act):
        for step in range(1, n_y):
            @pl.when(row > 0)
            def _(step=step):
                act(cross_pass(step, row - 1, 0))

            @pl.when(row < n_row - 1)
            def _(step=step):
                act(cross_pass(step, row + 1, 1))

    def cross_arrived():
        for step in range(1, n_y):
            source = y_column(step) // 2
            pltpu.make_async_copy(
                cross.at[source], cross.at[source], cross_recv.at[source]
            ).wait()

    def y_column(step):
        return lax.rem(y_own + step, n_y) * 2 + core

    near = jnp.minimum(row, n_row - 1 - row)
    lower = row > n_row - 1 - row

    def order(k):
        both = k < 2 * near
        step = jnp.where(both, k // 2 + 1, k - near + 1)
        down = jnp.where(both, k % 2 == 0, lower)
        return jnp.where(down, row - step, row + step)

    barrier = pltpu.get_barrier_semaphore()

    @pl.when(row > 0)
    def _():
        pl.semaphore_signal(barrier, inc=1, device_id={"row": row - 1}, device_id_type=MESH)

    @pl.when(row < n_row - 1)
    def _():
        pl.semaphore_signal(barrier, inc=1, device_id={"row": row + 1}, device_id_type=MESH)

    for step in range(1, n_y):
        pl.semaphore_signal(
            barrier, inc=1, device_id={"patch": y_column(step)}, device_id_type=MESH
        )
    pl.semaphore_signal(barrier, inc=1, device_id={"patch": sibling}, device_id_type=MESH)
    loads = [
        pltpu.make_async_copy(tok_hbm, tok, load_sem.at[0]),
        pltpu.make_async_copy(mod_hbm, mod, load_sem.at[1]),
    ]
    kv_width = 2 * width // KV_PARTS
    kv_loads = [
        pltpu.make_async_copy(
            wkv_hbm.at[:, pl.ds(i * kv_width, kv_width)],
            wkv.at[:, pl.ds(i * kv_width, kv_width)],
            kv_sem.at[i],
        )
        for i in range(KV_PARTS)
    ]
    wq_load = pltpu.make_async_copy(wq_hbm, wq, load_sem.at[2])
    wo_load = pltpu.make_async_copy(wo_hbm, wo, load_sem.at[3])
    for item in loads:
        item.start()

    pl.semaphore_wait(
        barrier,
        n_y + jnp.where(row > 0, 1, 0) + jnp.where(row < n_row - 1, 1, 0),
    )

    def z_copy(src, group, which, sem, target):
        return pltpu.make_async_remote_copy(
            src_ref=half(src, which), dst_ref=half(slot(group, patch), which), send_sem=sem,
            recv_sem=(key_sem, recv_sem)[which].at[group, patch], device_id={"row": target},
            device_id_type=MESH,
        )

    def first_event(act):
        for which in range(2):
            @pl.when(row > 0)
            def _(which=which):
                act(z_copy(stale_hbm, row, which, first_sem.at[0, which], row - 1))

            @pl.when(row < n_row - 1)
            def _(which=which):
                act(z_copy(stale_hbm, row, which, first_sem.at[1, which], row + 1))

    first_event(lambda copy: copy.start())

    for step in range(1, n_y):
        cross_send_copy(step).start()

    def y_send(group, step, adjacent):
        part = slot(group, patch)
        if adjacent:
            part = half(part, 1)
        return pltpu.make_async_remote_copy(
            src_ref=part, dst_ref=part, send_sem=y_sem.at[group, step],
            recv_sem=recv_sem.at[group, patch], device_id={"patch": y_column(step)},
            device_id_type=MESH,
        )

    def spread(group, adjacent=False):
        for step in range(1, n_y):
            y_send(group, step, adjacent).start()
        send(slot(group, patch), group, patch, core_sem.at[group, 0], {"patch": sibling}).start()

    def spread_wait(group, adjacent=False):
        for step in range(1, n_y):
            y_send(group, step, adjacent).wait_send()
        for step in range(n_y):
            send(slot(group, patch), group, patch, core_sem.at[group, step],
                 {"patch": sibling}).wait_send()

    def passed(distance, sign, act):
        group = row + sign * distance
        target = row - sign

        @pl.when((group >= 0) & (group < n_row))
        def _():
            act(group, (target >= 0) & (target < n_row), [
                z_copy(slot(group, patch), group, which, z_sem.at[group, which], target)
                for which in range(2)
            ])

    def row_event(distance, adjacent=False):
        def act(group, inside, copies):
            for which in range(2):
                part = half(slot(group, patch), which)
                pltpu.make_async_copy(
                    part, part, (key_sem, recv_sem)[which].at[group, patch]
                ).wait()

                @pl.when(inside)
                def _(which=which):
                    copies[which].start()

            spread(group, adjacent)

        passed(distance, 1, act)
        passed(distance, -1, act)

    def relay(group):
        for step in range(1, n_y):
            column = y_column(step)
            adjacent = (group == row - 1) | (group == row + 1)

            @pl.when(adjacent)
            def _(column=column):
                part = half(slot(group, column), 1)
                pltpu.make_async_copy(part, part, recv_sem.at[group, column]).wait()
                part = half(slot(group, column), 0)
                pltpu.make_async_copy(part, part, key_sem.at[group, column]).wait()

            @pl.when(jnp.logical_not(adjacent))
            def _(column=column):
                arrived(group, column)

            send(slot(group, column), group, column, core_sem.at[group, step],
                 {"patch": sibling}).start()

    def gathered(group):
        for step in range(n_y):
            arrived(group, y_column(step) + 1 - 2 * core)

    for item in kv_loads + [wq_load, wo_load]:
        item.start()

    for item in loads:
        item.wait()
    values = tok[...].astype(F32)
    center = jnp.mean(values, axis=-1, keepdims=True)
    offset = values - center
    spread_sq = jnp.mean(offset * offset, axis=-1, keepdims=True)
    normal = offset * lax.rsqrt(spread_sq + 1e-06)
    normed[...] = (normal * (1.0 + mod[1:2, :]) + mod[0:1, :]).astype(BF16)

    cell = lax.broadcasted_iota(jnp.int32, (block, tokens), 0)
    token = lax.broadcasted_iota(jnp.int32, (block, tokens), 1)
    home = (token // (2 * grid_cols)) * (grid_cols // 2) + (token % grid_cols) // 2
    pool = jnp.where(home == cell, 0.25, 0.0).astype(BF16)
    pooled = jnp.dot(pool, normed[...], preferred_element_type=F32)
    coarse = pooled.astype(BF16)
    fine = (pooled - coarse.astype(F32)).astype(BF16)
    both_parts = jnp.concatenate([coarse, fine], axis=0)
    own = slot(row, patch)
    for i in range(KV_PARTS):
        if i == 2:
            cross_arrived()
            cross_event(lambda copy: copy.start())
        kv_loads[i].wait()
        columns = pl.ds(i * kv_width, kv_width)
        product = jnp.dot(both_parts, wkv[:, columns], preferred_element_type=F32)
        own[:, columns] = (product[:block] + product[block:]).astype(BF16)
    spread(row)
    fresh_copy = pltpu.make_async_copy(own, fresh_hbm, fresh_sem)
    fresh_copy.start()

    if n_row > 1:
        row_event(1, True)

    wq_load.wait()
    lane = lax.broadcasted_iota(jnp.int32, (tokens, WINDOW), 1)

    def in_head(pair, which):
        begin = pair * (2 * HEAD_DIM - LANES) + which * HEAD_DIM
        return (lane >= begin) & (lane < begin + HEAD_DIM)

    query = jnp.dot(normed[...], wq[...], preferred_element_type=F32)
    for pair in range(PAIRS):
        window = query[:, pair * LANES : pair * LANES + WINDOW]
        for which in range(2):
            pair_q[pair, which * tokens : (which + 1) * tokens, :] = jnp.where(
                in_head(pair, which), window, 0.0
            ).astype(BF16)

    top[...] = jnp.full(top.shape, -1e30, F32)
    total[...] = jnp.zeros(total.shape, F32)
    summed[...] = jnp.zeros(summed.shape, F32)
    factor = math.log2(math.e) / math.sqrt(HEAD_DIM)

    def attend(start):
        rows = pl.ds(pl.multiple_of(start, LANES), LANES)
        for pair in range(PAIRS):
            keys = kv[rows, pair * LANES : pair * LANES + WINDOW]
            vals = kv[rows, width + pair * LANES : width + pair * LANES + WINDOW]
            scores = lax.dot_general(
                pair_q[pair], keys, (((1,), (1,)), ((), ())), preferred_element_type=F32
            )
            before = top[pair]
            newest = jnp.maximum(before, jnp.max(scores, axis=-1, keepdims=True))
            top[pair] = newest
            scale = jnp.exp2((before - newest) * factor)
            expo = jnp.exp2((scores - newest) * factor)
            total[pair] = total[pair] * scale + expo
            added = jnp.dot(expo.astype(BF16), vals, preferred_element_type=F32)
            summed[pair] = summed[pair] * jnp.concatenate([scale, scale], axis=1) + added

    group_rows = n_patch * block

    def step_group(q, carry):
        group = jnp.where(q == 0, row, order(jnp.maximum(q - 1, 0)))
        @pl.when(q > 0)
        def _():
            relay(group)

        @pl.when(q + 2 < n_row)
        def _():
            row_event(q + 2)

        @pl.when(q == 0)
        def _():
            relay(group)

        gathered(group)

        def step_part(u, state):
            attend(group * group_rows + u * LANES)
            return state

        return lax.fori_loop(0, group_rows // LANES, step_part, carry)

    lax.fori_loop(0, n_row, step_group, 0)

    attended[...] = jnp.zeros(attended.shape, F32)
    for pair in range(PAIRS):
        scaled = summed[pair] * (1.0 / jnp.sum(total[pair], axis=-1, keepdims=True))
        columns = slice(pair * LANES, pair * LANES + WINDOW)
        attended[:, columns] += jnp.where(
            in_head(pair, 0), scaled[:tokens], jnp.where(in_head(pair, 1), scaled[tokens:], 0.0)
        )
    wo_load.wait()
    heads = attended[...].astype(BF16)
    projected = jnp.dot(heads, wo[...], preferred_element_type=F32)
    out_ref[...] = (tok[...].astype(F32) + mod[2:3, :] * projected).astype(BF16)

    first_event(lambda copy: copy.wait_send())

    def finish(distance, carry, adjacent=False):
        def act(group, inside, copies):
            @pl.when(inside)
            def _():
                for copy in copies:
                    copy.wait_send()

            spread_wait(group, adjacent)

        passed(distance, 1, act)
        passed(distance, -1, act)
        return carry

    if n_row > 1:
        finish(1, 0, True)
    lax.fori_loop(2, n_row, finish, 0)
    for step in range(1, n_y):
        cross_send_copy(step).wait_send()
    cross_event(lambda copy: copy.wait_send())
    spread_wait(row)
    fresh_copy.wait()


def place(first, second, first_out, second_out, first_held, second_held, sem):
    loads = [
        pltpu.make_async_copy(first, first_held, sem.at[0]),
        pltpu.make_async_copy(second, second_held, sem.at[1]),
    ]
    stores = [
        pltpu.make_async_copy(first_held, first_out, sem.at[2]),
        pltpu.make_async_copy(second_held, second_out, sem.at[3]),
    ]
    for item in loads:
        item.start()
    for load, store in zip(loads, stores):
        load.wait()
        store.start()
    for item in stores:
        item.wait()


def on_device(n_row, n_patch, tokens, modulation, w_query, w_keyval, w_out, stale_kv):
    grid_rows, grid_cols, width = tokens.shape
    count = grid_rows * grid_cols
    block = count // 4
    dma = pltpu.SemaphoreType.DMA
    out, fresh = pl.pallas_call(
        functools.partial(kernel, n_row, n_patch, grid_cols),
        out_shape=(
            jax.ShapeDtypeStruct((count, width), BF16),
            jax.ShapeDtypeStruct((block, 2 * width), BF16),
        ),
        in_specs=[pl.BlockSpec(memory_space=pl.ANY)] * 6,
        out_specs=(
            pl.BlockSpec(memory_space=pltpu.VMEM),
            pl.BlockSpec(memory_space=pl.ANY),
        ),
        scratch_shapes=[
            pltpu.VMEM((count, width), BF16),
            pltpu.VMEM(modulation.shape, F32),
            pltpu.VMEM((width, width), BF16),
            pltpu.VMEM((width, 2 * width), BF16),
            pltpu.VMEM((width, width), BF16),
            pltpu.VMEM((n_row * n_patch * block, 2 * width), BF16),
            pltpu.VMEM((count, width), BF16),
            pltpu.VMEM((PAIRS, 2 * count, WINDOW), BF16),
            pltpu.VMEM((PAIRS, 2 * count, LANES), F32),
            pltpu.VMEM((PAIRS, 2 * count, LANES), F32),
            pltpu.VMEM((PAIRS, 2 * count, WINDOW), F32),
            pltpu.VMEM((count, width), F32),
            pltpu.VMEM((n_patch // 2, block, width), BF16),
            dma((4,)),
            dma((KV_PARTS,)),
            dma((n_row, n_patch)),
            dma((n_row, n_patch)),
            dma((n_patch // 2,)),
            dma((n_patch // 2,)),
            dma((2, n_patch // 2)),
            dma((2, 2)),
            dma((n_row, 2)),
            dma((n_row, n_patch // 2)),
            dma((n_row, n_patch // 2)),
            dma(()),
        ],
        compiler_params=pltpu.CompilerParams(
            collective_id=0, has_side_effects=True, vmem_limit_bytes=56 * 1024 * 1024
        ),
    )(
        tokens.reshape(count, width), modulation, w_query, w_keyval, w_out,
        stale_kv.reshape(block, 2 * width),
    )
    hbm = pl.BlockSpec(memory_space=pl.ANY)
    out, fresh = pl.pallas_call(
        place,
        out_shape=(
            jax.ShapeDtypeStruct(out.shape, BF16),
            jax.ShapeDtypeStruct(fresh.shape, BF16),
        ),
        in_specs=[hbm, hbm],
        out_specs=(hbm, hbm),
        scratch_shapes=[pltpu.VMEM(out.shape, BF16), pltpu.VMEM(fresh.shape, BF16), dma((4,))],
        compiler_params=pltpu.CompilerParams(vmem_limit_bytes=56 * 1024 * 1024),
    )(out, fresh)
    return out.reshape(tokens.shape), fresh.reshape(stale_kv.shape)


def solution(mesh):
    tiled = P(("rep", "row"), "patch", None)
    return jax.shard_map(
        functools.partial(on_device, mesh.shape["row"], mesh.shape["patch"]),
        mesh=mesh,
        in_specs=(tiled, P(), P(), P(), P(), tiled),
        out_specs=(tiled, tiled),
        check_vma=False,
    )
```
